256 devices in a mesh: ctx: 32 (over z, y), head: 8 (over x, core).
Axes of the slice: x: 4, y: 4, z: 8, core: 2. Of those that a mesh axis runs over, the one named last changes fastest.
Arguments:
- token_queries: bfloat16 [8192, 8192], P(('ctx', 'head')), may hold values from -4.5 to 4.5
- token_keys: bfloat16 [8192, 1024], P(('ctx', 'head')), may hold values from -4.5 to 4.5
- token_values: bfloat16 [8192, 1024], P(('ctx', 'head')), may hold values from -6 to 6
- doc_lengths: int32 [16], replicated, may hold values from 1 to 4096, 8192 in all
Outputs:
- attended: bfloat16 [8192, 8192], P(('ctx', 'head'))
The draws below stay inside these ranges and needn't reach their ends.
Inputs may be any that keep to these rules, and one draw needn't show every extreme that they name: `doc_lengths`: the lengths sum to 8192; the longest is exactly 4096.
All inputs are finite; a program needn't handle non-finite values.
Results may differ from the reference program's by a relative error of at most 0.0035.
Values may be sent and summed in bfloat16 or wider, within the bound.
A program may use at most 64 MiB of HBM per device.

```python
import math
import jax
import jax.numpy as jnp
import numpy as np
from jax import lax

QUERY_HEADS = 64
KEY_VALUE_HEADS = 8
HEAD_SIZE = 128
PACKED_TOKENS = 8192
LONGEST_TOKENS = 4096
DOCS = 16


def draw_token_queries(key, part):
    return jnp.clip(jax.random.normal(jax.random.fold_in(key, 22), (PACKED_TOKENS, QUERY_HEADS * HEAD_SIZE), jnp.float32), -4.5, 4.5).astype(jnp.bfloat16)


def draw_token_keys(key, part):
    return jnp.clip(jax.random.normal(jax.random.fold_in(key, 32), (PACKED_TOKENS, KEY_VALUE_HEADS * HEAD_SIZE), jnp.float32), -4.5, 4.5).astype(jnp.bfloat16)


def shard_levels(key, extent, cuts, least, high):
    loudness = 1.0
    for dim, shards_of in cuts:
        steps = jax.random.uniform(jax.random.fold_in(jax.random.fold_in(key, 6), dim), (shards_of,), jnp.float32, least / len(cuts), high / len(cuts))
        loudness = loudness * jnp.repeat(jnp.exp(steps), extent[dim] // shards_of).reshape((-1,) + (1,) * (len(extent) - 1 - dim))
    return loudness


def profile(count, total, reach, skew):
    loads = [(1 << 20) // math.isqrt(standing ** skew) + 1 for standing in range(2, count + 1)]
    spare, counts = total - reach - (count - 1), [1] * (count - 1)
    while spare > 0:
        free = [i for i in range(count - 1) if counts[i] < reach]
        whole, left = sum([loads[i] for i in free]), spare
        for i in free:
            extra = min(reach - counts[i], max(1, left * loads[i] // whole), spare)
            counts[i] = counts[i] + extra
            spare = spare - extra
    return np.array([reach] + counts)


def uneven(own_key, amount, total, limit, lean):
    if amount == 2:
        one = jax.random.randint(own_key, (), max(1, total - limit), min(limit, total - 1) + 1)
        return jnp.stack([one, total - one])
    tallies = jnp.asarray(profile(amount, total, limit, lean), jnp.int32)
    twos = (amount - 1) // 2
    source_of, receiver = tallies[1:1 + 2 * twos:2], tallies[2:2 + 2 * twos:2]
    room = jnp.minimum(source_of - 1, limit - receiver)
    shifted = jax.random.randint(jax.random.fold_in(own_key, 1), (twos,), 0, 1 << 20) % (room + 1)
    tallies = tallies.at[1:1 + 2 * twos:2].set(source_of - shifted).at[2:2 + 2 * twos:2].set(receiver + shifted)
    return tallies[jax.random.permutation(jax.random.fold_in(own_key, 2), amount)]


def centred(key, shape, width, limit, cuts=(), held_as=jnp.bfloat16):
    loudness = shard_levels(key, shape, cuts, -0.22, 0.18) if cuts else 1.0
    values = jax.random.normal(key, shape, jnp.float32) * width * loudness
    return jnp.minimum(jnp.maximum(values, -limit), limit).astype(held_as)


def setup_inputs(seed: int = 0) -> dict:
    seeds = jax.random.split(jax.random.key(seed), 5)
    token_queries = draw_token_queries(jax.random.fold_in(seeds[4], 71), 0)
    token_keys = draw_token_keys(jax.random.fold_in(seeds[4], 71), 0)
    token_values = centred(seeds[2], (PACKED_TOKENS, KEY_VALUE_HEADS * HEAD_SIZE), 1.0, 6.0, ((0, 256),))
    doc_lengths = uneven(seeds[3], DOCS, PACKED_TOKENS, LONGEST_TOKENS, 2).astype(jnp.int32)
    return dict(token_queries=token_queries, token_keys=token_keys, token_values=token_values, doc_lengths=doc_lengths)


def document_index(positions, bounds):
    return jnp.sum((bounds[None, :] <= positions[:, None]).astype(jnp.int32), axis=1)


def reference(token_queries, token_keys, token_values, doc_lengths):
    negative_big = -1e30
    bounds = jnp.cumsum(doc_lengths).astype(jnp.int32)
    positions = jnp.arange(PACKED_TOKENS, dtype=jnp.int32)
    documents = document_index(positions, bounds)
    group_factor = QUERY_HEADS // KEY_VALUE_HEADS
    query_matrix = token_queries.reshape(PACKED_TOKENS, KEY_VALUE_HEADS, group_factor, HEAD_SIZE).astype(jnp.float32)
    padding_amount = jnp.zeros((LONGEST_TOKENS, KEY_VALUE_HEADS, HEAD_SIZE), jnp.float32)
    keys_padded = jnp.concatenate([padding_amount, token_keys.reshape(PACKED_TOKENS, KEY_VALUE_HEADS, HEAD_SIZE).astype(jnp.float32)], axis=0)
    values_padded = jnp.concatenate([padding_amount, token_values.reshape(PACKED_TOKENS, KEY_VALUE_HEADS, HEAD_SIZE).astype(jnp.float32)], axis=0)
    padded_docs = jnp.concatenate([jnp.full((LONGEST_TOKENS,), -1, jnp.int32), documents], axis=0)
    padded_pos = jnp.concatenate([jnp.arange(LONGEST_TOKENS, dtype=jnp.int32) - LONGEST_TOKENS, positions], axis=0)
    block_rows = math.gcd(PACKED_TOKENS, 256)
    window = LONGEST_TOKENS + block_rows
    score_scale = HEAD_SIZE ** -0.5

    def one_block(block_index):
        offset = (block_index * block_rows).astype(jnp.int32)
        query_block = lax.dynamic_slice_in_dim(query_matrix, offset, block_rows, 0)
        query_docs = lax.dynamic_slice_in_dim(documents, offset, block_rows, 0)
        query_pos = lax.dynamic_slice_in_dim(positions, offset, block_rows, 0)
        key_block = lax.dynamic_slice_in_dim(keys_padded, offset, window, 0)
        value_block = lax.dynamic_slice_in_dim(values_padded, offset, window, 0)
        key_docs = lax.dynamic_slice_in_dim(padded_docs, offset, window, 0)
        key_pos = lax.dynamic_slice_in_dim(padded_pos, offset, window, 0)
        scores = jnp.einsum('qgrd,kgd->qgrk', query_block, key_block, precision=lax.Precision.HIGHEST) * score_scale
        allowed = (query_docs[:, None] == key_docs[None, :]) & (key_pos[None, :] <= query_pos[:, None])
        allowed = allowed[:, None, None, :]
        masked = jnp.where(allowed, scores, negative_big)
        row_max = jnp.max(masked, axis=-1, keepdims=True)
        weights = jnp.where(allowed, jnp.exp(masked - row_max), 0.0)
        weight_sum = jnp.sum(weights, axis=-1)
        rounded = lax.optimization_barrier(weights.astype(jnp.bfloat16)).astype(jnp.float32)
        combined = jnp.einsum('qgrk,kgd->qgrd', rounded, value_block, precision=lax.Precision.HIGHEST)
        return (combined / weight_sum[..., None]).reshape(block_rows, QUERY_HEADS * HEAD_SIZE).astype(jnp.bfloat16)

    blocks_out = lax.map(one_block, jnp.arange(PACKED_TOKENS // block_rows, dtype=jnp.int32))
    return blocks_out.reshape(PACKED_TOKENS, QUERY_HEADS * HEAD_SIZE)
```

```python
import functools

import jax
import jax.numpy as jnp
from jax import lax
from jax.experimental import pallas as pl
from jax.experimental.pallas import tpu as pltpu
from jax.sharding import PartitionSpec as P

QUERY_HEADS = 64
KEY_VALUE_HEADS = 8
HEAD_SIZE = 128
DOCS = 16
ROWS = 32
SUPER = 512
HALF = 256
SLOTS = 9
HEADS = 4
WIDE = HEADS * HEAD_SIZE
SCALE2 = HEAD_SIZE ** (-0.5) * 1.4426950408889634
NEGATIVE = -1e30
MESH = pl.DeviceIdType.MESH


def kernel(q_ref, k_ref, v_ref, doc_ref, o_ref, qbuf, kbuf, vbuf, kdoc, qdoc, acc, top, obuf,
           kv_send, kv_recv, q_send, q_recv, z_send, z_recv, y_send, y_recv, s_send, s_recv, o_send, o_recv):
    ctx, head = lax.axis_index("ctx"), lax.axis_index("head")
    z, y = ctx // 4, ctx % 4
    core = head % 2
    yp, yl = y // 2, y % 2
    after, before = lax.rem(z + 1, 8) * 4 + y, lax.rem(z + 7, 8) * 4 + y
    across = z * 4 + 3 - y
    other = head + 1 - 2 * core
    here = z * 8 + head + yl * 256
    me = yl * 8 + head

    def member(i):
        return z * 4 + 2 * yp + i // 8, i % 8

    def heads_of(i):
        parity = (i // 8 + yp) % 2
        group = 2 * ((i % 8) // 2) + parity
        return group, group * 8 + (i % 2) * HEADS

    barrier = pltpu.get_barrier_semaphore()

    def greet(i, _):
        to = lax.rem(me + i, 16)
        c, h = member(to)
        pl.semaphore_signal(barrier, inc=1, device_id=(c, h), device_id_type=MESH)
        return 0

    lax.fori_loop(1, 16, greet, 0)
    for c in (after, before, across):
        pl.semaphore_signal(barrier, inc=1, device_id=(c, head), device_id_type=MESH)
    pl.semaphore_wait(barrier, 18)

    def remote(src, dst, send, recv, to):
        return pltpu.make_async_remote_copy(src_ref=src, dst_ref=dst, send_sem=send, recv_sem=recv,
                                            device_id=to, device_id_type=MESH)

    my_rows = pl.multiple_of(me * ROWS, ROWS)

    def kv_target(j):
        return (j * 2 + yl)

    def kv_copy(j, part, start):
        to = kv_target(j)
        group, _ = heads_of(to)
        ref, buf = ((k_ref, kbuf), (v_ref, vbuf))[part]
        src = ref.at[:, pl.ds(pl.multiple_of(group * HEAD_SIZE, HEAD_SIZE), HEAD_SIZE)]
        dst = buf.at[pl.ds(my_rows, ROWS), :]

        @pl.when(to != me)
        def _():
            copy = remote(src, dst, kv_send.at[part, j], kv_recv.at[part, head], member(to))
            if start:
                copy.start()
            else:
                copy.wait_send()

        if start:
            @pl.when(to == me)
            def _():
                pltpu.make_async_copy(src, dst, kv_recv.at[part, head]).start()

    def kv_arrive(j, part):
        buf = (kbuf, vbuf)[part]
        rows = pl.ds(pl.multiple_of((core * 8 + j) * ROWS, ROWS), ROWS)
        pltpu.make_async_copy(buf.at[rows, :], buf.at[rows, :], kv_recv.at[part, j]).wait()

    def q_copy(i, start):
        to = lax.rem(me + i, 16)
        _, first = heads_of(to)
        src = q_ref.at[:, pl.ds(pl.multiple_of(first * HEAD_SIZE, WIDE), WIDE)]
        dst = qbuf.at[pl.ds(my_rows, ROWS), :]
        copy = remote(src, dst, q_send.at[to], q_recv.at[me], member(to))
        if start:
            copy.start()
        else:
            copy.wait_send()

    def q_own():
        _, first = heads_of(me)
        src = q_ref.at[:, pl.ds(pl.multiple_of(first * HEAD_SIZE, WIDE), WIDE)]
        return pltpu.make_async_copy(src, qbuf.at[pl.ds(my_rows, ROWS), :], q_recv.at[me])

    def q_arrive(i):
        rows = pl.ds(pl.multiple_of(i * ROWS, ROWS), ROWS)
        pltpu.make_async_copy(qbuf.at[rows, :], qbuf.at[rows, :], q_recv.at[i]).wait()

    def loop(n, f, first=0):
        def body(i, _):
            f(i)
            return 0
        lax.fori_loop(first, n, body, 0)

    def piece(buf, slot, half):
        return buf.at[pl.ds(pl.multiple_of(slot * SUPER + half * HALF, HALF), HALF), :]

    def z_copy(d, part):
        buf = (kbuf, vbuf)[part]
        return remote(piece(buf, 2 * d, core), piece(buf, 2 * d + 2, core), z_send.at[part, d],
                      z_recv.at[part, d + 1], (after, head))

    def y_copy(i, part):
        buf = (kbuf, vbuf)[part]
        return remote(piece(buf, 2 * (i + yp), core), piece(buf, 2 * i + 1, core), y_send.at[part, i],
                      y_recv.at[part, i], (across, head))

    def s_copy(slot, part):
        buf = (kbuf, vbuf)[part]
        return remote(piece(buf, slot, core), piece(buf, slot, core), s_send.at[part, slot],
                      s_recv.at[part, slot], (ctx, other))

    def landed(slot, half, sem, part):
        buf = (kbuf, vbuf)[part]
        ref = piece(buf, slot, half)
        pltpu.make_async_copy(ref, ref, sem).wait()

    def pass_on(d):
        for part in (0, 1):
            if d > 0:
                landed(2 * d, core, z_recv.at[part, d], part)
            if d < 4:
                z_copy(d, part).start()

            @pl.when((d - yp >= 0) & (d - yp < 4))
            def _():
                y_copy(jnp.clip(d - yp, 0, 3), part).start()

            s_copy(2 * d, part).start()

    def pass_odd(i):
        for part in (0, 1):
            landed(2 * i + 1, core, y_recv.at[part, i], part)
            s_copy(2 * i + 1, part).start()

    def whole(slot):
        for part in (0, 1):
            landed(slot, 1 - core, s_recv.at[part, slot], part)

    def o_copy(g, i):
        to = lax.rem(me + i, 16)
        _, first = heads_of(me)
        src = obuf.at[g, pl.ds(pl.multiple_of(to * ROWS, ROWS), ROWS), :]
        dst = o_ref.at[:, pl.ds(pl.multiple_of((first + g) * HEAD_SIZE, HEAD_SIZE), HEAD_SIZE)]
        return remote(src, dst, o_send.at[g, to], o_recv.at[g, me], member(to))

    def o_own(g):
        _, first = heads_of(me)
        src = obuf.at[g, pl.ds(my_rows, ROWS), :]
        dst = o_ref.at[:, pl.ds(pl.multiple_of((first + g) * HEAD_SIZE, HEAD_SIZE), HEAD_SIZE)]
        return pltpu.make_async_copy(src, dst, o_recv.at[g, me])

    def o_arrive(g, i):
        _, first = heads_of(i)
        dst = o_ref.at[:, pl.ds(pl.multiple_of((first + g) * HEAD_SIZE, HEAD_SIZE), HEAD_SIZE)]
        pltpu.make_async_copy(dst, dst, o_recv.at[g, i]).wait()

    for part in (0, 1):
        loop(8, lambda j: kv_copy(j, part, True))
    q_own().start()
    loop(16, lambda i: q_copy(i, True), 1)

    lane = lax.broadcasted_iota(jnp.int32, (1, HEAD_SIZE), 1)
    begins = jnp.where(lane == DOCS, -(1 << 20), 1 << 20)
    ends = jnp.where(lane == DOCS, 0, 1 << 20)
    total = jnp.int32(0)
    for j in range(DOCS):
        begins = jnp.where(lane == j, total, begins)
        total = total + doc_ref[j]
        ends = jnp.where(lane == j, total, ends)
    base = (z * 2 + yp) * SUPER

    def one_hot(first, count):
        position = first + lax.broadcasted_iota(jnp.int32, (count, HEAD_SIZE), 0)
        return (position >= begins) & (position < ends)

    qdoc[...] = jnp.where(one_hot(base, SUPER), 0.0, NEGATIVE).astype(jnp.bfloat16)

    def key_documents(slot):
        kdoc[pl.ds(pl.multiple_of(slot * SUPER, SUPER), SUPER), :] = jnp.where(
            one_hot(base - slot * SUPER, SUPER), 1.0, 0.0).astype(jnp.bfloat16)

    loop(SLOTS, key_documents)

    def attend(g, first_slot, slots, kind):
        keys = slots * SUPER
        rows = pl.ds(first_slot * SUPER, keys)
        q = jnp.concatenate([qbuf[:, pl.ds(pl.multiple_of(g * HEAD_SIZE, HEAD_SIZE), HEAD_SIZE)], qdoc[...]], axis=1)
        k = jnp.concatenate([kbuf[rows, :], kdoc[rows, :]], axis=1)
        v = jnp.concatenate([vbuf[rows, :], jnp.ones((keys, HEAD_SIZE), jnp.bfloat16)], axis=1)
        s = lax.dot_general(q, k, (((1,), (1,)), ((), ())), preferred_element_type=jnp.float32)
        if kind != "middle":
            t = lax.broadcasted_iota(jnp.int32, (SUPER, keys), 0)
            u = lax.broadcasted_iota(jnp.int32, (SUPER, keys), 1)
            if kind == "first":
                s = jnp.where(u <= t, s, NEGATIVE)
            else:
                s = jnp.where(u > t + (keys - SUPER), s, NEGATIVE) if slots == 1 else jnp.where(
                    (u < SUPER) | (u - SUPER > t), s, NEGATIVE)
        high = jnp.max(s, axis=1, keepdims=True)
        if kind != "first":
            old = top[g][:, :1]
            high = jnp.maximum(high, old)
        p = jnp.exp2(s * SCALE2 - high * SCALE2).astype(jnp.bfloat16)
        part = jnp.dot(p, v, preferred_element_type=jnp.float32)
        if kind != "first":
            part = part + acc[g] * jnp.exp2((old - high) * SCALE2)
        if kind == "last":
            obuf[g] = (part[:, :HEAD_SIZE] / part[:, HEAD_SIZE:]).astype(jnp.bfloat16)
        else:
            acc[g] = part
            top[g] = jnp.broadcast_to(high, (SUPER, HEAD_SIZE))

    def pair(n, first_slot, slots, kind):
        for g in (2 * n, 2 * n + 1):
            attend(g, first_slot, slots, kind)

    for part in (0, 1):
        loop(8, lambda j: kv_arrive(j, part))
    pass_on(0)
    loop(16, q_arrive)
    whole(0)
    pair(0, 0, 1, "first")
    pass_on(1)
    pair(1, 0, 1, "first")
    pass_odd(0)
    for i in range(1, 5):
        whole(2 * i)
        whole(2 * i - 1)
        kind = "last" if i == 4 else "middle"
        pair(0, 2 * i - 1, 2, kind)
        if i < 4:
            pass_on(i + 1)
        else:
            for g in (0, 1):
                o_own(g).start()
                loop(16, lambda j: o_copy(g, j).start(), 1)
        pair(1, 2 * i - 1, 2, kind)
        if i < 4:
            pass_odd(i)
    for g in (2, 3):
        o_own(g).start()
        loop(16, lambda j: o_copy(g, j).start(), 1)

    for part in (0, 1):
        loop(8, lambda j: kv_copy(j, part, False))
        for d in range(4):
            z_copy(d, part).wait_send()
            y_copy(d, part).wait_send()
        for slot in range(SLOTS):
            s_copy(slot, part).wait_send()
    loop(16, lambda i: q_copy(i, False), 1)
    for g in range(HEADS):
        loop(16, lambda j: o_copy(g, j).wait_send(), 1)
        loop(16, lambda i: o_arrive(g, i))


def on_device(token_queries, token_keys, token_values, doc_lengths):
    dma = pltpu.SemaphoreType.DMA
    any_space = pl.BlockSpec(memory_space=pl.ANY)
    return pl.pallas_call(
        kernel,
        name="packed_attention",
        out_shape=jax.ShapeDtypeStruct((ROWS, QUERY_HEADS * HEAD_SIZE), jnp.bfloat16),
        in_specs=[any_space] * 3 + [pl.BlockSpec(memory_space=pltpu.SMEM)],
        out_specs=any_space,
        scratch_shapes=[
            pltpu.VMEM((SUPER, WIDE), jnp.bfloat16),
            pltpu.VMEM((SLOTS * SUPER, HEAD_SIZE), jnp.bfloat16),
            pltpu.VMEM((SLOTS * SUPER, HEAD_SIZE), jnp.bfloat16),
            pltpu.VMEM((SLOTS * SUPER, HEAD_SIZE), jnp.bfloat16),
            pltpu.VMEM((SUPER, HEAD_SIZE), jnp.bfloat16),
            pltpu.VMEM((HEADS, SUPER, 2 * HEAD_SIZE), jnp.float32),
            pltpu.VMEM((HEADS, SUPER, HEAD_SIZE), jnp.float32),
            pltpu.VMEM((HEADS, SUPER, HEAD_SIZE), jnp.bfloat16),
            dma((2, 8)), dma((2, 8)), dma((16,)), dma((16,)),
            dma((2, 4)), dma((2, 5)), dma((2, 4)), dma((2, 4)),
            dma((2, SLOTS)), dma((2, SLOTS)), dma((HEADS, 16)), dma((HEADS, 16)),
        ],
        compiler_params=pltpu.CompilerParams(
            collective_id=0, has_side_effects=True, vmem_limit_bytes=52 * 2**20),
    )(token_queries, token_keys, token_values, doc_lengths)


def solution(mesh):
    in_specs = (P(("ctx", "head"), None), P(("ctx", "head"), None), P(("ctx", "head"), None), P())
    return jax.shard_map(
        on_device, mesh=mesh, in_specs=in_specs, out_specs=P(("ctx", "head"), None), check_vma=False
    )
```

```python
import functools

import jax
import jax.numpy as jnp
from jax import lax
from jax.experimental import pallas as pl
from jax.experimental.pallas import tpu as pltpu
from jax.sharding import PartitionSpec as P

QUERY_HEADS = 64
KEY_VALUE_HEADS = 8
HEAD_SIZE = 128
DOCS = 16
ROWS = 32
SUPER = 512
HALF = 256
SLOTS = 9
HEADS = 4
SCALE2 = HEAD_SIZE ** (-0.5) * 1.4426950408889634
NEGATIVE = -1e30
MESH = pl.DeviceIdType.MESH


def kernel(q_ref, k_ref, v_ref, doc_ref, o_ref, qbuf, kbuf, vbuf, kdoc, qdoc, acc, top, obuf,
           kv_send, kv_recv, q_send, q_recv, z_send, z_recv, y_send, y_recv, s_send, s_recv, o_send, o_recv):
    ctx, head = lax.axis_index("ctx"), lax.axis_index("head")
    z, y = ctx // 4, ctx % 4
    core = head % 2
    yp, yl = y // 2, y % 2
    after, before = lax.rem(z + 1, 8) * 4 + y, lax.rem(z + 7, 8) * 4 + y
    across = z * 4 + 3 - y
    other = head + 1 - 2 * core
    me = yl * 8 + head

    def member(i):
        return z * 4 + 2 * yp + i // 8, i % 8

    def heads_of(i):
        parity = (i // 8 + yp) % 2
        group = 2 * ((i % 8) // 2) + parity
        return group, group * 8 + (i % 2) * HEADS

    barrier = pltpu.get_barrier_semaphore()

    def greet(i, _):
        to = lax.rem(me + i, 16)
        c, h = member(to)
        pl.semaphore_signal(barrier, inc=1, device_id=(c, h), device_id_type=MESH)
        return 0

    lax.fori_loop(1, 16, greet, 0)
    for c in (after, before, across):
        pl.semaphore_signal(barrier, inc=1, device_id=(c, head), device_id_type=MESH)
    pl.semaphore_wait(barrier, 18)

    def remote(src, dst, send, recv, to):
        return pltpu.make_async_remote_copy(src_ref=src, dst_ref=dst, send_sem=send, recv_sem=recv,
                                            device_id=to, device_id_type=MESH)

    my_rows = pl.multiple_of(me * ROWS, ROWS)

    def kv_target(j):
        return (j * 2 + yl)

    def kv_copy(j, part, start):
        to = kv_target(j)
        group, _ = heads_of(to)
        ref, buf = ((k_ref, kbuf), (v_ref, vbuf))[part]
        src = ref.at[:, pl.ds(pl.multiple_of(group * HEAD_SIZE, HEAD_SIZE), HEAD_SIZE)]
        dst = buf.at[pl.ds(my_rows, ROWS), :]

        @pl.when(to != me)
        def _():
            copy = remote(src, dst, kv_send.at[part, j], kv_recv.at[part, head], member(to))
            if start:
                copy.start()
            else:
                copy.wait_send()

        if start:
            @pl.when(to == me)
            def _():
                pltpu.make_async_copy(src, dst, kv_recv.at[part, head]).start()

    def kv_arrive(j, part):
        buf = (kbuf, vbuf)[part]
        rows = pl.ds(pl.multiple_of((core * 8 + j) * ROWS, ROWS), ROWS)
        pltpu.make_async_copy(buf.at[rows, :], buf.at[rows, :], kv_recv.at[part, j]).wait()

    def q_copy(n, i, start):
        to = lax.rem(me + i, 16)
        _, first = heads_of(to)
        src = q_ref.at[:, pl.ds(pl.multiple_of((first + 2 * n) * HEAD_SIZE, 2 * HEAD_SIZE), 2 * HEAD_SIZE)]
        dst = qbuf.at[n, pl.ds(my_rows, ROWS), :]
        copy = remote(src, dst, q_send.at[n, to], q_recv.at[n, me], member(to))
        if start:
            copy.start()
        else:
            copy.wait_send()

    def q_own(n):
        _, first = heads_of(me)
        src = q_ref.at[:, pl.ds(pl.multiple_of((first + 2 * n) * HEAD_SIZE, 2 * HEAD_SIZE), 2 * HEAD_SIZE)]
        return pltpu.make_async_copy(src, qbuf.at[n, pl.ds(my_rows, ROWS), :], q_recv.at[n, me])

    def q_arrive(n, i):
        rows = pl.ds(pl.multiple_of(i * ROWS, ROWS), ROWS)
        pltpu.make_async_copy(qbuf.at[n, rows, :], qbuf.at[n, rows, :], q_recv.at[n, i]).wait()

    def loop(n, f, first=0):
        def body(i, _):
            f(i)
            return 0
        lax.fori_loop(first, n, body, 0)

    def piece(buf, slot, half):
        return buf.at[pl.ds(pl.multiple_of(slot * SUPER + half * HALF, HALF), HALF), :]

    def z_copy(d, part):
        buf = (kbuf, vbuf)[part]
        return remote(piece(buf, 2 * d, core), piece(buf, 2 * d + 2, core), z_send.at[part, d],
                      z_recv.at[part, d + 1], (after, head))

    def y_copy(i, part):
        buf = (kbuf, vbuf)[part]
        return remote(piece(buf, 2 * (i + yp), core), piece(buf, 2 * i + 1, core), y_send.at[part, i],
                      y_recv.at[part, i], (across, head))

    def s_copy(slot, part):
        buf = (kbuf, vbuf)[part]
        return remote(piece(buf, slot, core), piece(buf, slot, core), s_send.at[part, slot],
                      s_recv.at[part, slot], (ctx, other))

    def landed(slot, half, sem, part):
        buf = (kbuf, vbuf)[part]
        ref = piece(buf, slot, half)
        pltpu.make_async_copy(ref, ref, sem).wait()

    def pass_on(d):
        for part in (0, 1):
            if d > 0:
                landed(2 * d, core, z_recv.at[part, d], part)
            if d < 4:
                z_copy(d, part).start()

            @pl.when((d - yp >= 0) & (d - yp < 4))
            def _():
                y_copy(jnp.clip(d - yp, 0, 3), part).start()

            s_copy(2 * d, part).start()

    def pass_odd(i):
        for part in (0, 1):
            landed(2 * i + 1, core, y_recv.at[part, i], part)
            s_copy(2 * i + 1, part).start()

    def whole(slot):
        for part in (0, 1):
            landed(slot, 1 - core, s_recv.at[part, slot], part)

    def o_copy(n, i):
        to = lax.rem(me + i, 16)
        _, first = heads_of(me)
        src = obuf.at[n, pl.ds(pl.multiple_of(to * ROWS, ROWS), ROWS), :]
        dst = o_ref.at[:, pl.ds(pl.multiple_of((first + 2 * n) * HEAD_SIZE, 2 * HEAD_SIZE), 2 * HEAD_SIZE)]
        return remote(src, dst, o_send.at[n, to], o_recv.at[n, me], member(to))

    def o_own(n):
        _, first = heads_of(me)
        src = obuf.at[n, pl.ds(my_rows, ROWS), :]
        dst = o_ref.at[:, pl.ds(pl.multiple_of((first + 2 * n) * HEAD_SIZE, 2 * HEAD_SIZE), 2 * HEAD_SIZE)]
        return pltpu.make_async_copy(src, dst, o_recv.at[n, me])

    def o_arrive(n, i):
        _, first = heads_of(i)
        dst = o_ref.at[:, pl.ds(pl.multiple_of((first + 2 * n) * HEAD_SIZE, 2 * HEAD_SIZE), 2 * HEAD_SIZE)]
        pltpu.make_async_copy(dst, dst, o_recv.at[n, i]).wait()

    def o_send_pair(n):
        o_own(n).start()
        loop(16, lambda j: o_copy(n, j).start(), 1)

    for part in (0, 1):
        loop(8, lambda j: kv_copy(j, part, True))
    for n in (0, 1):
        q_own(n).start()
        loop(16, lambda i: q_copy(n, i, True), 1)

    lane = lax.broadcasted_iota(jnp.int32, (1, HEAD_SIZE), 1)
    begins = jnp.where(lane == DOCS, -(1 << 20), 1 << 20)
    ends = jnp.where(lane == DOCS, 0, 1 << 20)
    total = jnp.int32(0)
    for j in range(DOCS):
        begins = jnp.where(lane == j, total, begins)
        total = total + doc_ref[j]
        ends = jnp.where(lane == j, total, ends)
    base = (z * 2 + yp) * SUPER

    def one_hot(first, count):
        position = first + lax.broadcasted_iota(jnp.int32, (count, HEAD_SIZE), 0)
        return (position >= begins) & (position < ends)

    qdoc[...] = jnp.where(one_hot(base, SUPER), 0.0, NEGATIVE).astype(jnp.bfloat16)

    def key_documents(slot):
        kdoc[pl.ds(pl.multiple_of(slot * SUPER, SUPER), SUPER), :] = jnp.where(
            one_hot(base - slot * SUPER, SUPER), 1.0, 0.0).astype(jnp.bfloat16)

    loop(SLOTS, key_documents)

    def attend(g, first_slot, slots, kind):
        keys = slots * SUPER
        rows = pl.ds(first_slot * SUPER, keys)
        q = jnp.concatenate([qbuf[g // 2, :, (g % 2) * HEAD_SIZE : (g % 2 + 1) * HEAD_SIZE], qdoc[...]], axis=1)
        k = jnp.concatenate([kbuf[rows, :], kdoc[rows, :]], axis=1)
        v = jnp.concatenate([vbuf[rows, :], jnp.ones((keys, HEAD_SIZE), jnp.bfloat16)], axis=1)
        s = lax.dot_general(q, k, (((1,), (1,)), ((), ())), preferred_element_type=jnp.float32)
        if kind != "middle":
            t = lax.broadcasted_iota(jnp.int32, (SUPER, keys), 0)
            u = lax.broadcasted_iota(jnp.int32, (SUPER, keys), 1)
            if kind == "first":
                s = jnp.where(u <= t, s, NEGATIVE)
            else:
                s = jnp.where(u > t + (keys - SUPER), s, NEGATIVE) if slots == 1 else jnp.where(
                    (u < SUPER) | (u - SUPER > t), s, NEGATIVE)
        high = jnp.max(s, axis=1, keepdims=True)
        if kind != "first":
            old = top[g][:, :1]
            high = jnp.maximum(high, old)
        p = jnp.exp2(s * SCALE2 - high * SCALE2).astype(jnp.bfloat16)
        part = jnp.dot(p, v, preferred_element_type=jnp.float32)
        if kind != "first":
            part = part + acc[g] * jnp.exp2((old - high) * SCALE2)
        if kind == "last":
            obuf[g // 2, :, (g % 2) * HEAD_SIZE : (g % 2 + 1) * HEAD_SIZE] = (part[:, :HEAD_SIZE] / part[:, HEAD_SIZE:]).astype(jnp.bfloat16)
        else:
            acc[g] = part
            top[g] = jnp.broadcast_to(high, (SUPER, HEAD_SIZE))

    def pair(n, first_slot, slots, kind):
        for g in (2 * n, 2 * n + 1):
            attend(g, first_slot, slots, kind)

    for part in (0, 1):
        loop(8, lambda j: kv_arrive(j, part))
    pass_on(0)
    whole(0)
    pass_on(1)
    loop(16, lambda i: q_arrive(0, i))
    pair(0, 0, 1, "first")
    loop(16, lambda i: q_arrive(1, i))
    pair(1, 0, 1, "first")
    pass_on(2)
    pass_odd(0)
    for i in range(1, 5):
        whole(2 * i)
        whole(2 * i - 1)
        kind = "last" if i == 4 else "middle"
        pair(0, 2 * i - 1, 2, kind)
        if i < 3:
            pass_on(i + 2)
        if i < 4:
            pass_odd(i)
        else:
            o_send_pair(0)
        pair(1, 2 * i - 1, 2, kind)
    o_send_pair(1)

    for part in (0, 1):
        loop(8, lambda j: kv_copy(j, part, False))
        for d in range(4):
            z_copy(d, part).wait_send()
            y_copy(d, part).wait_send()
        for slot in range(SLOTS):
            s_copy(slot, part).wait_send()
    for n in (0, 1):
        loop(16, lambda i: q_copy(n, i, False), 1)
    for n in (0, 1):
        loop(16, lambda j: o_copy(n, j).wait_send(), 1)
        loop(16, lambda i: o_arrive(n, i))


def on_device(token_queries, token_keys, token_values, doc_lengths):
    dma = pltpu.SemaphoreType.DMA
    any_space = pl.BlockSpec(memory_space=pl.ANY)
    return pl.pallas_call(
        kernel,
        name="packed_attention",
        out_shape=jax.ShapeDtypeStruct((ROWS, QUERY_HEADS * HEAD_SIZE), jnp.bfloat16),
        in_specs=[any_space] * 3 + [pl.BlockSpec(memory_space=pltpu.SMEM)],
        out_specs=any_space,
        scratch_shapes=[
            pltpu.VMEM((2, SUPER, 2 * HEAD_SIZE), jnp.bfloat16),
            pltpu.VMEM((SLOTS * SUPER, HEAD_SIZE), jnp.bfloat16),
            pltpu.VMEM((SLOTS * SUPER, HEAD_SIZE), jnp.bfloat16),
            pltpu.VMEM((SLOTS * SUPER, HEAD_SIZE), jnp.bfloat16),
            pltpu.VMEM((SUPER, HEAD_SIZE), jnp.bfloat16),
            pltpu.VMEM((HEADS, SUPER, 2 * HEAD_SIZE), jnp.float32),
            pltpu.VMEM((HEADS, SUPER, HEAD_SIZE), jnp.float32),
            pltpu.VMEM((2, SUPER, 2 * HEAD_SIZE), jnp.bfloat16),
            dma((2, 8)), dma((2, 8)), dma((2, 16)), dma((2, 16)),
            dma((2, 4)), dma((2, 5)), dma((2, 4)), dma((2, 4)),
            dma((2, SLOTS)), dma((2, SLOTS)), dma((2, 16)), dma((2, 16)),
        ],
        compiler_params=pltpu.CompilerParams(
            collective_id=0, has_side_effects=True, vmem_limit_bytes=63 * 2**20),
    )(token_queries, token_keys, token_values, doc_lengths)


def solution(mesh):
    in_specs = (P(("ctx", "head"), None), P(("ctx", "head"), None), P(("ctx", "head"), None), P())
    return jax.shard_map(
        on_device, mesh=mesh, in_specs=in_specs, out_specs=P(("ctx", "head"), None), check_vma=False
    )
```

```python
import functools

import jax
import jax.numpy as jnp
from jax import lax
from jax.experimental import pallas as pl
from jax.experimental.pallas import tpu as pltpu
from jax.sharding import PartitionSpec as P

QUERY_HEADS = 64
KEY_VALUE_HEADS = 8
HEAD_SIZE = 128
DOCS = 16
ROWS = 32
SUPER = 512
HALF = 256
LEVELS = 8
SLOTS = 9
HEADS = 4
SCALE2 = HEAD_SIZE ** (-0.5) * 1.4426950408889634
NEGATIVE = -1e30
MESH = pl.DeviceIdType.MESH


def kernel(q_ref, k_ref, v_ref, doc_ref, o_ref, qbuf, kbuf, vbuf, kdoc, qdoc, acc, top, obuf,
           kv_send, kv_recv, q_send, q_recv, z_send, z_recv, y_send, y_recv, s_send, s_recv, o_send, o_recv, q_in, k_in, v_in, in_sem):
    ctx, head = lax.axis_index("ctx"), lax.axis_index("head")
    z, y = ctx // 4, ctx % 4
    core = head % 2
    yp, yl = y // 2, y % 2
    after, before = jnp.minimum(z + 1, LEVELS - 1) * 4 + y, jnp.maximum(z - 1, 0) * 4 + y
    across = z * 4 + 3 - y
    other = head + 1 - 2 * core
    me = yl * 8 + head

    def member(i):
        return z * 4 + 2 * yp + i // 8, i % 8

    def heads_of(i):
        parity = (i // 8 + yp) % 2
        group = 2 * ((i % 8) // 2) + parity
        return group, group * 8 + (i % 2) * HEADS

    fetch = [pltpu.make_async_copy(src, dst, in_sem.at[i])
             for i, (src, dst) in enumerate(((k_ref, k_in), (v_ref, v_in), (q_ref, q_in)))]
    for copy in fetch:
        copy.start()

    barrier = pltpu.get_barrier_semaphore()

    def greet(i, _):
        to = lax.rem(me + i, 16)
        c, h = member(to)
        pl.semaphore_signal(barrier, inc=1, device_id=(c, h), device_id_type=MESH)
        return 0

    lax.fori_loop(1, 16, greet, 0)
    pl.semaphore_signal(barrier, inc=1, device_id=(across, head), device_id_type=MESH)

    @pl.when(z < LEVELS - 1)
    def _():
        pl.semaphore_signal(barrier, inc=1, device_id=(after, head), device_id_type=MESH)

    @pl.when(z > 0)
    def _():
        pl.semaphore_signal(barrier, inc=1, device_id=(before, head), device_id_type=MESH)

    pl.semaphore_wait(barrier, 18 - (z == 0).astype(jnp.int32) - (z == LEVELS - 1).astype(jnp.int32))

    for copy in fetch:
        copy.wait()

    def remote(src, dst, send, recv, to):
        return pltpu.make_async_remote_copy(src_ref=src, dst_ref=dst, send_sem=send, recv_sem=recv,
                                            device_id=to, device_id_type=MESH)

    my_rows = pl.multiple_of(me * ROWS, ROWS)

    def kv_target(j):
        return (j * 2 + yl)

    def kv_copy(j, part, start):
        to = kv_target(j)
        group, _ = heads_of(to)
        ref, buf = ((k_in, kbuf), (v_in, vbuf))[part]
        src = ref.at[:, pl.ds(pl.multiple_of(group * HEAD_SIZE, HEAD_SIZE), HEAD_SIZE)]
        dst = buf.at[pl.ds(my_rows, ROWS), :]

        @pl.when(to != me)
        def _():
            copy = remote(src, dst, kv_send.at[part, j], kv_recv.at[part, head], member(to))
            if start:
                copy.start()
            else:
                copy.wait_send()

        if start:
            @pl.when(to == me)
            def _():
                pltpu.make_async_copy(src, dst, kv_recv.at[part, head]).start()

    def kv_arrive(j, part):
        buf = (kbuf, vbuf)[part]
        rows = pl.ds(pl.multiple_of((core * 8 + j) * ROWS, ROWS), ROWS)
        pltpu.make_async_copy(buf.at[rows, :], buf.at[rows, :], kv_recv.at[part, j]).wait()

    def q_copy(n, i, start):
        to = lax.rem(me + i, 16)
        _, first = heads_of(to)
        src = q_in.at[:, pl.ds(pl.multiple_of((first + 2 * n) * HEAD_SIZE, 2 * HEAD_SIZE), 2 * HEAD_SIZE)]
        dst = qbuf.at[n, pl.ds(my_rows, ROWS), :]
        copy = remote(src, dst, q_send.at[n, to], q_recv.at[n, me], member(to))
        if start:
            copy.start()
        else:
            copy.wait_send()

    def q_own(n):
        _, first = heads_of(me)
        src = q_in.at[:, pl.ds(pl.multiple_of((first + 2 * n) * HEAD_SIZE, 2 * HEAD_SIZE), 2 * HEAD_SIZE)]
        return pltpu.make_async_copy(src, qbuf.at[n, pl.ds(my_rows, ROWS), :], q_recv.at[n, me])

    def q_arrive(n, i):
        rows = pl.ds(pl.multiple_of(i * ROWS, ROWS), ROWS)
        pltpu.make_async_copy(qbuf.at[n, rows, :], qbuf.at[n, rows, :], q_recv.at[n, i]).wait()

    def loop(n, f, first=0):
        def body(i, _):
            f(i)
            return 0
        lax.fori_loop(first, n, body, 0)

    def piece(buf, slot, half):
        return buf.at[pl.ds(pl.multiple_of(slot * SUPER + half * HALF, HALF), HALF), :]

    def z_copy(d, part):
        buf = (kbuf, vbuf)[part]
        return remote(piece(buf, 2 * d, core), piece(buf, 2 * d + 2, core), z_send.at[part, d],
                      z_recv.at[part, d + 1], (after, head))

    def y_copy(i, part):
        buf = (kbuf, vbuf)[part]
        return remote(piece(buf, 2 * (i + yp), core), piece(buf, 2 * i + 1, core), y_send.at[part, i],
                      y_recv.at[part, i], (across, head))

    def s_copy(slot, part):
        buf = (kbuf, vbuf)[part]
        return remote(piece(buf, slot, core), piece(buf, slot, core), s_send.at[part, slot],
                      s_recv.at[part, slot], (ctx, other))

    def landed(slot, half, sem, part):
        buf = (kbuf, vbuf)[part]
        ref = piece(buf, slot, half)
        pltpu.make_async_copy(ref, ref, sem).wait()

    def back_copy(n):
        if n == 0:
            return remote(piece(kbuf, 0, core), around, b_send.at[0], b_recv.at[0], (back, head))
        return remote(around, piece(kbuf, 8, core), b_send.at[1], z_recv.at[0, 4], (back, head))

    def exists(slot):
        return 2 * z + yp >= slot

    def pass_on(d, parts=(0, 1)):
        @pl.when(exists(2 * d))
        def _():
            for part in parts:
                if d > 0:
                    landed(2 * d, core, z_recv.at[part, d], part)
                if d < 4:
                    @pl.when(z < LEVELS - 1)
                    def _():
                        z_copy(d, part).start()
                if d == 0:
                    @pl.when(yp == 0)
                    def _():
                        y_copy(0, part).start()
                elif d == 4:
                    @pl.when(yp == 1)
                    def _():
                        y_copy(3, part).start()
                else:
                    y_copy(d - yp, part).start()
                s_copy(2 * d, part).start()

    def pass_odd(i):
        @pl.when(exists(2 * i + 1))
        def _():
            for part in (0, 1):
                landed(2 * i + 1, core, y_recv.at[part, i], part)
                s_copy(2 * i + 1, part).start()

    def whole(slot):
        @pl.when(exists(slot))
        def _():
            for part in (0, 1):
                landed(slot, 1 - core, s_recv.at[part, slot], part)

    def o_copy(n, i):
        to = lax.rem(me + i, 16)
        _, first = heads_of(me)
        src = obuf.at[n, pl.ds(pl.multiple_of(to * ROWS, ROWS), ROWS), :]
        dst = o_ref.at[:, pl.ds(pl.multiple_of((first + 2 * n) * HEAD_SIZE, 2 * HEAD_SIZE), 2 * HEAD_SIZE)]
        return remote(src, dst, o_send.at[n, to], o_recv.at[n, me], member(to))

    def o_own(n):
        _, first = heads_of(me)
        src = obuf.at[n, pl.ds(my_rows, ROWS), :]
        dst = o_ref.at[:, pl.ds(pl.multiple_of((first + 2 * n) * HEAD_SIZE, 2 * HEAD_SIZE), 2 * HEAD_SIZE)]
        return pltpu.make_async_copy(src, dst, o_recv.at[n, me])

    def o_arrive(n, i):
        _, first = heads_of(i)
        dst = o_ref.at[:, pl.ds(pl.multiple_of((first + 2 * n) * HEAD_SIZE, 2 * HEAD_SIZE), 2 * HEAD_SIZE)]
        pltpu.make_async_copy(dst, dst, o_recv.at[n, i]).wait()

    def o_send_pair(n):
        o_own(n).start()
        loop(16, lambda j: o_copy(n, j).start(), 1)

    for part in (0, 1):
        loop(8, lambda j: kv_copy(j, part, True))
    for n in (0, 1):
        q_own(n).start()
        loop(16, lambda i: q_copy(n, i, True), 1)

    lane = lax.broadcasted_iota(jnp.int32, (1, HEAD_SIZE), 1)
    begins = jnp.where(lane == DOCS, -(1 << 20), 1 << 20)
    ends = jnp.where(lane == DOCS, 0, 1 << 20)
    total = jnp.int32(0)
    for j in range(DOCS):
        begins = jnp.where(lane == j, total, begins)
        total = total + doc_ref[j]
        ends = jnp.where(lane == j, total, ends)
    base = (z * 2 + yp) * SUPER

    def one_hot(first, count):
        position = first + lax.broadcasted_iota(jnp.int32, (count, HEAD_SIZE), 0)
        return (position >= begins) & (position < ends)

    qdoc[...] = jnp.where(one_hot(base, SUPER), 0.0, NEGATIVE).astype(jnp.bfloat16)

    def key_documents(slot):
        kdoc[pl.ds(pl.multiple_of(slot * SUPER, SUPER), SUPER), :] = jnp.where(
            one_hot(base - slot * SUPER, SUPER), 1.0, 0.0).astype(jnp.bfloat16)

    loop(SLOTS, key_documents)
    for slot in range(1, SLOTS):
        @pl.when(jnp.logical_not(exists(slot)))
        def _():
            for buf in (kbuf, vbuf):
                buf[pl.ds(slot * SUPER, SUPER), :] = jnp.zeros((SUPER, HEAD_SIZE), jnp.bfloat16)

    def attend(g, r, slots, kind):
        blocks = []
        for slot in slots:
            if slot == 0:
                blocks = [(0, r)] + ([(0, 0)] if r == 1 else []) + blocks
            elif slot == 8:
                blocks = [(8, r)] + ([(8, 1)] if r == 0 else []) + blocks
            else:
                blocks = blocks + [(slot, 0), (slot, 1)]
        keys = len(blocks) * HALF
        mine = pl.ds(r * HALF, HALF)

        def rows_of(ref):
            return jnp.concatenate([ref[pl.ds(slot * SUPER + half * HALF, HALF), :] for slot, half in blocks], axis=0)

        q = jnp.concatenate(
            [qbuf[g // 2, mine, (g % 2) * HEAD_SIZE : (g % 2 + 1) * HEAD_SIZE], qdoc[mine, :]], axis=1)
        k = jnp.concatenate([rows_of(kbuf), rows_of(kdoc)], axis=1)
        v = jnp.concatenate([rows_of(vbuf), jnp.ones((keys, HEAD_SIZE), jnp.bfloat16)], axis=1)
        s = lax.dot_general(q, k, (((1,), (1,)), ((), ())), preferred_element_type=jnp.float32)
        if 0 in slots or 8 in slots:
            t = lax.broadcasted_iota(jnp.int32, (HALF, HALF), 0)
            u = lax.broadcasted_iota(jnp.int32, (HALF, HALF), 1)
            near = jnp.where(u <= t if 0 in slots else u > t, s[:, :HALF], NEGATIVE)
            s = jnp.concatenate([near, s[:, HALF:]], axis=1)
        high = jnp.max(s, axis=1, keepdims=True)
        if kind != "first":
            old = top[g, mine, :1]
            high = jnp.maximum(high, old)
        p = jnp.exp2(s * SCALE2 - high * SCALE2).astype(jnp.bfloat16)
        part = jnp.dot(p, v, preferred_element_type=jnp.float32)
        if kind != "first":
            part = part + acc[g, mine, :] * jnp.exp2((old - high) * SCALE2)
        if kind == "last":
            obuf[g // 2, mine, (g % 2) * HEAD_SIZE : (g % 2 + 1) * HEAD_SIZE] = (
                part[:, :HEAD_SIZE] / part[:, HEAD_SIZE:]).astype(jnp.bfloat16)
        else:
            acc[g, mine, :] = part
            top[g, mine, :] = jnp.broadcast_to(high, (HALF, HEAD_SIZE))

    def pair(n, slots, kind="middle"):
        def run():
            for g in (2 * n, 2 * n + 1):
                for r in (0, 1):
                    attend(g, r, slots, kind)

        if kind == "middle":
            pl.when(exists(min(slots)))(run)
        else:
            run()

    for part in (0, 1):
        loop(8, lambda j: kv_arrive(j, part))
    pass_on(0)
    pass_on(1)
    whole(0)
    whole(2)
    loop(16, lambda i: q_arrive(0, i))
    pair(0, (0, 2), "first")
    loop(16, lambda i: q_arrive(1, i))
    pass_on(2)
    pass_odd(0)
    pair(1, (0, 2), "first")
    whole(1)
    whole(4)
    pair(0, (1, 4))
    pass_on(3)
    pass_odd(1)
    pair(1, (1, 4))
    whole(3)
    whole(6)
    pair(0, (3, 6))
    pass_on(4)
    pass_odd(2)
    pair(1, (3, 6))
    whole(8)
    whole(5)
    pair(0, (8, 5))
    pass_odd(3)
    whole(7)
    pair(0, (7,), "last")
    o_send_pair(0)
    pair(1, (8, 5, 7), "last")
    o_send_pair(1)

    for part in (0, 1):
        loop(8, lambda j: kv_copy(j, part, False))
        for d in range(4):
            @pl.when(exists(2 * d) & (z < LEVELS - 1))
            def _():
                z_copy(d, part).wait_send()

            @pl.when(z >= d + yp)
            def _():
                y_copy(d, part).wait_send()
        for slot in range(SLOTS):
            @pl.when(exists(slot))
            def _():
                s_copy(slot, part).wait_send()
    for n in (0, 1):
        loop(16, lambda i: q_copy(n, i, False), 1)
    for n in (0, 1):
        loop(16, lambda j: o_copy(n, j).wait_send(), 1)
        loop(16, lambda i: o_arrive(n, i))


def on_device(token_queries, token_keys, token_values, doc_lengths):
    dma = pltpu.SemaphoreType.DMA
    any_space = pl.BlockSpec(memory_space=pl.ANY)
    return pl.pallas_call(
        kernel,
        name="packed_attention",
        out_shape=jax.ShapeDtypeStruct((ROWS, QUERY_HEADS * HEAD_SIZE), jnp.bfloat16),
        in_specs=[any_space] * 3 + [pl.BlockSpec(memory_space=pltpu.SMEM)],
        out_specs=any_space,
        scratch_shapes=[
            pltpu.VMEM((2, SUPER, 2 * HEAD_SIZE), jnp.bfloat16),
            pltpu.VMEM((SLOTS * SUPER, HEAD_SIZE), jnp.bfloat16),
            pltpu.VMEM((SLOTS * SUPER, HEAD_SIZE), jnp.bfloat16),
            pltpu.VMEM((SLOTS * SUPER, HEAD_SIZE), jnp.bfloat16),
            pltpu.VMEM((SUPER, HEAD_SIZE), jnp.bfloat16),
            pltpu.VMEM((HEADS, SUPER, 2 * HEAD_SIZE), jnp.float32),
            pltpu.VMEM((HEADS, SUPER, HEAD_SIZE), jnp.float32),
            pltpu.VMEM((2, SUPER, 2 * HEAD_SIZE), jnp.bfloat16),
            dma((2, 8)), dma((2, 8)), dma((2, 16)), dma((2, 16)),
            dma((2, 4)), dma((2, 5)), dma((2, 4)), dma((2, 4)),
            dma((2, SLOTS)), dma((2, SLOTS)), dma((2, 16)), dma((2, 16)),
            pltpu.VMEM((ROWS, QUERY_HEADS * HEAD_SIZE), jnp.bfloat16),
            pltpu.VMEM((ROWS, KEY_VALUE_HEADS * HEAD_SIZE), jnp.bfloat16),
            pltpu.VMEM((ROWS, KEY_VALUE_HEADS * HEAD_SIZE), jnp.bfloat16),
            dma((3,)),
        ],
        compiler_params=pltpu.CompilerParams(
            collective_id=0, has_side_effects=True, vmem_limit_bytes=63 * 2**20),
    )(token_queries, token_keys, token_values, doc_lengths)


def solution(mesh):
    in_specs = (P(("ctx", "head"), None), P(("ctx", "head"), None), P(("ctx", "head"), None), P())
    return jax.shard_map(
        on_device, mesh=mesh, in_specs=in_specs, out_specs=P(("ctx", "head"), None), check_vma=False
    )
```

```python
import functools

import jax
import jax.numpy as jnp
from jax import lax
from jax.experimental import pallas as pl
from jax.experimental.pallas import tpu as pltpu
from jax.sharding import PartitionSpec as P

QUERY_HEADS = 64
KEY_VALUE_HEADS = 8
HEAD_SIZE = 128
DOCS = 16
ROWS = 32
SUPER = 512
HALF = 256
LEVELS = 8
SLOTS = 9
HEADS = 4
SCALE2 = HEAD_SIZE ** (-0.5) * 1.4426950408889634
NEGATIVE = -1e30
MESH = pl.DeviceIdType.MESH


def kernel(q_ref, k_ref, v_ref, doc_ref, o_ref, qbuf, kbuf, vbuf, kdoc, qdoc, acc, top, obuf,
           kv_send, kv_recv, q_send, q_recv, z_send, z_recv, y_send, y_recv, s_send, s_recv, o_send, o_recv, q_in, k_in, v_in, in_sem):
    ctx, head = lax.axis_index("ctx"), lax.axis_index("head")
    z, y = ctx // 4, ctx % 4
    core = head % 2
    yp, yl = y // 2, y % 2
    after, before = jnp.minimum(z + 1, LEVELS - 1) * 4 + y, jnp.maximum(z - 1, 0) * 4 + y
    across = z * 4 + 3 - y
    other = head + 1 - 2 * core
    me = yl * 8 + head

    def member(i):
        return z * 4 + 2 * yp + i // 8, i % 8

    def heads_of(i):
        parity = (i // 8 + yp) % 2
        group = 2 * ((i % 8) // 2) + parity
        return group, group * 8 + (i % 2) * HEADS

    fetch = [pltpu.make_async_copy(src, dst, in_sem.at[i])
             for i, (src, dst) in enumerate(((k_ref, k_in), (v_ref, v_in), (q_ref, q_in)))]
    for copy in fetch:
        copy.start()

    barrier = pltpu.get_barrier_semaphore()

    def greet(i, _):
        to = lax.rem(me + i, 16)
        c, h = member(to)
        pl.semaphore_signal(barrier, inc=1, device_id=(c, h), device_id_type=MESH)
        return 0

    lax.fori_loop(1, 16, greet, 0)
    pl.semaphore_signal(barrier, inc=1, device_id=(across, head), device_id_type=MESH)

    @pl.when(z < LEVELS - 1)
    def _():
        pl.semaphore_signal(barrier, inc=1, device_id=(after, head), device_id_type=MESH)

    @pl.when(z > 0)
    def _():
        pl.semaphore_signal(barrier, inc=1, device_id=(before, head), device_id_type=MESH)

    pl.semaphore_wait(barrier, 18 - (z == 0).astype(jnp.int32) - (z == LEVELS - 1).astype(jnp.int32))

    for copy in fetch:
        copy.wait()

    def remote(src, dst, send, recv, to):
        return pltpu.make_async_remote_copy(src_ref=src, dst_ref=dst, send_sem=send, recv_sem=recv,
                                            device_id=to, device_id_type=MESH)

    my_rows = pl.multiple_of(me * ROWS, ROWS)

    def kv_target(j):
        return (j * 2 + yl)

    def kv_copy(j, part, start):
        to = kv_target(j)
        group, _ = heads_of(to)
        ref, buf = ((k_in, kbuf), (v_in, vbuf))[part]
        src = ref.at[:, pl.ds(pl.multiple_of(group * HEAD_SIZE, HEAD_SIZE), HEAD_SIZE)]
        dst = buf.at[pl.ds(my_rows, ROWS), :]

        @pl.when(to != me)
        def _():
            copy = remote(src, dst, kv_send.at[part, j], kv_recv.at[part, head], member(to))
            if start:
                copy.start()
            else:
                copy.wait_send()

        if start:
            @pl.when(to == me)
            def _():
                pltpu.make_async_copy(src, dst, kv_recv.at[part, head]).start()

    def kv_arrive(j, part):
        buf = (kbuf, vbuf)[part]
        rows = pl.ds(pl.multiple_of((core * 8 + j) * ROWS, ROWS), ROWS)
        pltpu.make_async_copy(buf.at[rows, :], buf.at[rows, :], kv_recv.at[part, j]).wait()

    def q_copy(n, i, start):
        to = lax.rem(me + i, 16)
        _, first = heads_of(to)
        src = q_in.at[:, pl.ds(pl.multiple_of((first + 2 * n) * HEAD_SIZE, 2 * HEAD_SIZE), 2 * HEAD_SIZE)]
        dst = qbuf.at[n, pl.ds(my_rows, ROWS), :]
        copy = remote(src, dst, q_send.at[n, to], q_recv.at[n, me], member(to))
        if start:
            copy.start()
        else:
            copy.wait_send()

    def q_own(n):
        _, first = heads_of(me)
        src = q_in.at[:, pl.ds(pl.multiple_of((first + 2 * n) * HEAD_SIZE, 2 * HEAD_SIZE), 2 * HEAD_SIZE)]
        return pltpu.make_async_copy(src, qbuf.at[n, pl.ds(my_rows, ROWS), :], q_recv.at[n, me])

    def q_arrive(n, i):
        rows = pl.ds(pl.multiple_of(i * ROWS, ROWS), ROWS)
        pltpu.make_async_copy(qbuf.at[n, rows, :], qbuf.at[n, rows, :], q_recv.at[n, i]).wait()

    def loop(n, f, first=0):
        def body(i, _):
            f(i)
            return 0
        lax.fori_loop(first, n, body, 0)

    def piece(buf, slot, half):
        return buf.at[pl.ds(pl.multiple_of(slot * SUPER + half * HALF, HALF), HALF), :]

    def z_copy(d, part):
        buf = (kbuf, vbuf)[part]
        return remote(piece(buf, 2 * d, core), piece(buf, 2 * d + 2, core), z_send.at[part, d],
                      z_recv.at[part, d + 1], (after, head))

    def y_copy(i, part):
        buf = (kbuf, vbuf)[part]
        return remote(piece(buf, 2 * (i + yp), core), piece(buf, 2 * i + 1, core), y_send.at[part, i],
                      y_recv.at[part, i], (across, head))

    def s_copy(slot, part):
        buf = (kbuf, vbuf)[part]
        return remote(piece(buf, slot, core), piece(buf, slot, core), s_send.at[part, slot],
                      s_recv.at[part, slot], (ctx, other))

    def landed(slot, half, sem, part):
        buf = (kbuf, vbuf)[part]
        ref = piece(buf, slot, half)
        pltpu.make_async_copy(ref, ref, sem).wait()

    def back_copy(n):
        if n == 0:
            return remote(piece(kbuf, 0, core), around, b_send.at[0], b_recv.at[0], (back, head))
        return remote(around, piece(kbuf, 8, core), b_send.at[1], z_recv.at[0, 4], (back, head))

    def exists(slot):
        return 2 * z + yp >= slot

    def pass_on(d, parts=(0, 1)):
        @pl.when(exists(2 * d))
        def _():
            for part in parts:
                if d > 0:
                    landed(2 * d, core, z_recv.at[part, d], part)
                if d < 4:
                    @pl.when(z < LEVELS - 1)
                    def _():
                        z_copy(d, part).start()
                if d == 0:
                    @pl.when(yp == 0)
                    def _():
                        y_copy(0, part).start()
                elif d == 4:
                    @pl.when(yp == 1)
                    def _():
                        y_copy(3, part).start()
                else:
                    y_copy(d - yp, part).start()
                s_copy(2 * d, part).start()

    def pass_odd(i, parts=(0, 1)):
        @pl.when(exists(2 * i + 1))
        def _():
            for part in parts:
                landed(2 * i + 1, core, y_recv.at[part, i], part)
                s_copy(2 * i + 1, part).start()

    def whole(slot):
        @pl.when(exists(slot))
        def _():
            for part in (0, 1):
                landed(slot, 1 - core, s_recv.at[part, slot], part)

    def o_copy(n, i):
        to = lax.rem(me + i, 16)
        _, first = heads_of(me)
        src = obuf.at[n, pl.ds(pl.multiple_of(to * ROWS, ROWS), ROWS), :]
        dst = o_ref.at[:, pl.ds(pl.multiple_of((first + 2 * n) * HEAD_SIZE, 2 * HEAD_SIZE), 2 * HEAD_SIZE)]
        return remote(src, dst, o_send.at[n, to], o_recv.at[n, me], member(to))

    def o_own(n):
        _, first = heads_of(me)
        src = obuf.at[n, pl.ds(my_rows, ROWS), :]
        dst = o_ref.at[:, pl.ds(pl.multiple_of((first + 2 * n) * HEAD_SIZE, 2 * HEAD_SIZE), 2 * HEAD_SIZE)]
        return pltpu.make_async_copy(src, dst, o_recv.at[n, me])

    def o_arrive(n, i):
        _, first = heads_of(i)
        dst = o_ref.at[:, pl.ds(pl.multiple_of((first + 2 * n) * HEAD_SIZE, 2 * HEAD_SIZE), 2 * HEAD_SIZE)]
        pltpu.make_async_copy(dst, dst, o_recv.at[n, i]).wait()

    def o_send_pair(n):
        o_own(n).start()
        loop(16, lambda j: o_copy(n, j).start(), 1)

    for part in (0, 1):
        loop(8, lambda j: kv_copy(j, part, True))
    def q_send_pair(n):
        q_own(n).start()
        loop(16, lambda i: q_copy(n, i, True), 1)

    q_send_pair(0)

    lane = lax.broadcasted_iota(jnp.int32, (1, HEAD_SIZE), 1)
    begins = jnp.where(lane == DOCS, -(1 << 20), 1 << 20)
    ends = jnp.where(lane == DOCS, 0, 1 << 20)
    total = jnp.int32(0)
    for j in range(DOCS):
        begins = jnp.where(lane == j, total, begins)
        total = total + doc_ref[j]
        ends = jnp.where(lane == j, total, ends)
    base = (z * 2 + yp) * SUPER

    def one_hot(first, count):
        position = first + lax.broadcasted_iota(jnp.int32, (count, HEAD_SIZE), 0)
        return (position >= begins) & (position < ends)

    qdoc[...] = jnp.where(one_hot(base, SUPER), 0.0, NEGATIVE).astype(jnp.bfloat16)

    def key_documents(slot):
        kdoc[pl.ds(pl.multiple_of(slot * SUPER, SUPER), SUPER), :] = jnp.where(
            one_hot(base - slot * SUPER, SUPER), 1.0, 0.0).astype(jnp.bfloat16)

    loop(SLOTS, key_documents)
    for slot in range(1, SLOTS):
        @pl.when(jnp.logical_not(exists(slot)))
        def _():
            for buf in (kbuf, vbuf):
                buf[pl.ds(slot * SUPER, SUPER), :] = jnp.zeros((SUPER, HEAD_SIZE), jnp.bfloat16)

    def attend(g, r, slots, kind):
        blocks = []
        for slot in slots:
            if slot == 0:
                blocks = [(0, r)] + ([(0, 0)] if r == 1 else []) + blocks
            elif slot == 8:
                blocks = [(8, r)] + ([(8, 1)] if r == 0 else []) + blocks
            else:
                blocks = blocks + [(slot, 0), (slot, 1)]
        keys = len(blocks) * HALF
        mine = pl.ds(r * HALF, HALF)

        def rows_of(ref):
            parts = [ref[pl.ds(slot * SUPER + half * HALF, HALF), :] for slot, half in blocks]
            return parts[0] if len(parts) == 1 else jnp.concatenate(parts, axis=0)

        q = jnp.concatenate(
            [qbuf[g // 2, mine, (g % 2) * HEAD_SIZE : (g % 2 + 1) * HEAD_SIZE], qdoc[mine, :]], axis=1)
        k = jnp.concatenate([rows_of(kbuf), rows_of(kdoc)], axis=1)
        v = jnp.concatenate([rows_of(vbuf), jnp.ones((keys, HEAD_SIZE), jnp.bfloat16)], axis=1)
        s = lax.dot_general(q, k, (((1,), (1,)), ((), ())), preferred_element_type=jnp.float32)
        if 0 in slots or 8 in slots:
            t = lax.broadcasted_iota(jnp.int32, (HALF, HALF), 0)
            u = lax.broadcasted_iota(jnp.int32, (HALF, HALF), 1)
            near = jnp.where(u <= t if 0 in slots else u > t, s[:, :HALF], NEGATIVE)
            s = near if keys == HALF else jnp.concatenate([near, s[:, HALF:]], axis=1)
        high = jnp.max(s, axis=1, keepdims=True)
        if kind != "first":
            old = top[g, mine, :1]
            high = jnp.maximum(high, old)
        p = jnp.exp2(s * SCALE2 - high * SCALE2).astype(jnp.bfloat16)
        part = jnp.dot(p, v, preferred_element_type=jnp.float32)
        if kind != "first":
            part = part + acc[g, mine, :] * jnp.exp2((old - high) * SCALE2)
        if kind == "last":
            obuf[g // 2, mine, (g % 2) * HEAD_SIZE : (g % 2 + 1) * HEAD_SIZE] = (
                part[:, :HEAD_SIZE] / part[:, HEAD_SIZE:]).astype(jnp.bfloat16)
        else:
            acc[g, mine, :] = part
            top[g, mine, :] = jnp.broadcast_to(high, (HALF, HEAD_SIZE))

    def pair(n, slots, kind="middle"):
        def run():
            for g in (2 * n, 2 * n + 1):
                for r in (0, 1):
                    attend(g, r, slots, kind)

        if kind == "middle":
            pl.when(exists(min(slots)))(run)
        else:
            run()

    loop(8, lambda j: kv_arrive(j, 0))
    pass_on(0, (0,))
    q_send_pair(1)
    loop(8, lambda j: kv_arrive(j, 1))
    pass_on(0, (1,))
    pass_on(1, (0,))
    whole(0)
    pass_on(1, (1,))
    loop(16, lambda i: q_arrive(0, i))
    pair(0, (0,), "first")
    pass_on(2, (0,))
    whole(2)
    pair(0, (2,))
    pass_on(2, (1,))
    pass_on(3, (0,))
    pass_odd(0)
    loop(16, lambda i: q_arrive(1, i))
    pair(1, (0, 2), "first")
    pass_on(3, (1,))
    pass_on(4, (0,))
    pass_odd(1, (0,))
    whole(1)
    whole(4)
    pair(0, (1, 4))
    pass_on(4, (1,))
    pass_odd(1, (1,))
    pass_odd(2, (0,))
    pair(1, (1, 4))
    pass_odd(2, (1,))
    pass_odd(3, (0,))
    whole(3)
    whole(6)
    pair(0, (3, 6))
    pass_odd(3, (1,))
    pair(1, (3, 6))
    whole(8)
    whole(5)
    whole(7)
    pair(0, (8, 5, 7), "last")
    o_send_pair(0)
    pair(1, (8, 5, 7), "last")
    o_send_pair(1)

    for part in (0, 1):
        loop(8, lambda j: kv_copy(j, part, False))
        for d in range(4):
            @pl.when(exists(2 * d) & (z < LEVELS - 1))
            def _():
                z_copy(d, part).wait_send()

            @pl.when(z >= d + yp)
            def _():
                y_copy(d, part).wait_send()
        for slot in range(SLOTS):
            @pl.when(exists(slot))
            def _():
                s_copy(slot, part).wait_send()
    for n in (0, 1):
        loop(16, lambda i: q_copy(n, i, False), 1)
    for n in (0, 1):
        loop(16, lambda j: o_copy(n, j).wait_send(), 1)
        loop(16, lambda i: o_arrive(n, i))


def on_device(token_queries, token_keys, token_values, doc_lengths):
    dma = pltpu.SemaphoreType.DMA
    any_space = pl.BlockSpec(memory_space=pl.ANY)
    return pl.pallas_call(
        kernel,
        name="packed_attention",
        out_shape=jax.ShapeDtypeStruct((ROWS, QUERY_HEADS * HEAD_SIZE), jnp.bfloat16),
        in_specs=[any_space] * 3 + [pl.BlockSpec(memory_space=pltpu.SMEM)],
        out_specs=any_space,
        scratch_shapes=[
            pltpu.VMEM((2, SUPER, 2 * HEAD_SIZE), jnp.bfloat16),
            pltpu.VMEM((SLOTS * SUPER, HEAD_SIZE), jnp.bfloat16),
            pltpu.VMEM((SLOTS * SUPER, HEAD_SIZE), jnp.bfloat16),
            pltpu.VMEM((SLOTS * SUPER, HEAD_SIZE), jnp.bfloat16),
            pltpu.VMEM((SUPER, HEAD_SIZE), jnp.bfloat16),
            pltpu.VMEM((HEADS, SUPER, 2 * HEAD_SIZE), jnp.float32),
            pltpu.VMEM((HEADS, SUPER, HEAD_SIZE), jnp.float32),
            pltpu.VMEM((2, SUPER, 2 * HEAD_SIZE), jnp.bfloat16),
            dma((2, 8)), dma((2, 8)), dma((2, 16)), dma((2, 16)),
            dma((2, 4)), dma((2, 5)), dma((2, 4)), dma((2, 4)),
            dma((2, SLOTS)), dma((2, SLOTS)), dma((2, 16)), dma((2, 16)),
            pltpu.VMEM((ROWS, QUERY_HEADS * HEAD_SIZE), jnp.bfloat16),
            pltpu.VMEM((ROWS, KEY_VALUE_HEADS * HEAD_SIZE), jnp.bfloat16),
            pltpu.VMEM((ROWS, KEY_VALUE_HEADS * HEAD_SIZE), jnp.bfloat16),
            dma((3,)),
        ],
        compiler_params=pltpu.CompilerParams(
            collective_id=0, has_side_effects=True, vmem_limit_bytes=63 * 2**20),
    )(token_queries, token_keys, token_values, doc_lengths)


def solution(mesh):
    in_specs = (P(("ctx", "head"), None), P(("ctx", "head"), None), P(("ctx", "head"), None), P())
    return jax.shard_map(
        on_device, mesh=mesh, in_specs=in_specs, out_specs=P(("ctx", "head"), None), check_vma=False
    )
```

```python
import functools

import jax
import jax.numpy as jnp
from jax import lax
from jax.experimental import pallas as pl
from jax.experimental.pallas import tpu as pltpu
from jax.sharding import PartitionSpec as P

QUERY_HEADS = 64
KEY_VALUE_HEADS = 8
HEAD_SIZE = 128
DOCS = 16
ROWS = 32
SUPER = 512
HALF = 256
LEVELS = 8
SLOTS = 9
HEADS = 4
SCALE2 = HEAD_SIZE ** (-0.5) * 1.4426950408889634
NEGATIVE = -1e30
MESH = pl.DeviceIdType.MESH


def kernel(q_ref, k_ref, v_ref, doc_ref, o_ref, qbuf, kbuf, vbuf, kdoc, qdoc, acc, top, obuf,
           kv_send, kv_recv, q_send, q_recv, z_send, z_recv, y_send, y_recv, s_send, s_recv, o_send, o_recv, q_in, k_in, v_in, in_sem):
    ctx, head = lax.axis_index("ctx"), lax.axis_index("head")
    z, y = ctx // 4, ctx % 4
    core = head % 2
    yp, yl = y // 2, y % 2
    after, before = jnp.minimum(z + 1, LEVELS - 1) * 4 + y, jnp.maximum(z - 1, 0) * 4 + y
    across = z * 4 + 3 - y
    other = head + 1 - 2 * core
    me = yl * 8 + head

    def member(i):
        return z * 4 + 2 * yp + i // 8, i % 8

    def heads_of(i):
        parity = (i // 8 + yp) % 2
        group = 2 * ((i % 8) // 2) + parity
        return group, group * 8 + (i % 2) * HEADS

    fetch = [pltpu.make_async_copy(src, dst, in_sem.at[i])
             for i, (src, dst) in enumerate(((k_ref, k_in), (v_ref, v_in), (q_ref, q_in)))]
    for copy in fetch:
        copy.start()

    barrier = pltpu.get_barrier_semaphore()

    def greet(i, _):
        to = lax.rem(me + i, 16)
        c, h = member(to)
        pl.semaphore_signal(barrier, inc=1, device_id=(c, h), device_id_type=MESH)
        return 0

    lax.fori_loop(1, 16, greet, 0)
    pl.semaphore_signal(barrier, inc=1, device_id=(across, head), device_id_type=MESH)

    @pl.when(z < LEVELS - 1)
    def _():
        pl.semaphore_signal(barrier, inc=1, device_id=(after, head), device_id_type=MESH)

    @pl.when(z > 0)
    def _():
        pl.semaphore_signal(barrier, inc=1, device_id=(before, head), device_id_type=MESH)

    pl.semaphore_wait(barrier, 18 - (z == 0).astype(jnp.int32) - (z == LEVELS - 1).astype(jnp.int32))

    for copy in fetch[:2]:
        copy.wait()

    def remote(src, dst, send, recv, to):
        return pltpu.make_async_remote_copy(src_ref=src, dst_ref=dst, send_sem=send, recv_sem=recv,
                                            device_id=to, device_id_type=MESH)

    my_rows = pl.multiple_of(me * ROWS, ROWS)

    def kv_target(j):
        return (j * 2 + yl)

    def kv_copy(j, part, start):
        to = kv_target(j)
        group, _ = heads_of(to)
        ref, buf = ((k_in, kbuf), (v_in, vbuf))[part]
        src = ref.at[:, pl.ds(pl.multiple_of(group * HEAD_SIZE, HEAD_SIZE), HEAD_SIZE)]
        dst = buf.at[pl.ds(my_rows, ROWS), :]

        @pl.when(to != me)
        def _():
            copy = remote(src, dst, kv_send.at[part, j], kv_recv.at[part, head], member(to))
            if start:
                copy.start()
            else:
                copy.wait_send()

        if start:
            @pl.when(to == me)
            def _():
                pltpu.make_async_copy(src, dst, kv_recv.at[part, head]).start()

    def kv_arrive(j, part):
        buf = (kbuf, vbuf)[part]
        rows = pl.ds(pl.multiple_of((core * 8 + j) * ROWS, ROWS), ROWS)
        pltpu.make_async_copy(buf.at[rows, :], buf.at[rows, :], kv_recv.at[part, j]).wait()

    def q_copy(n, i, start):
        to = lax.rem(me + i, 16)
        _, first = heads_of(to)
        src = q_in.at[:, pl.ds(pl.multiple_of((first + 2 * n) * HEAD_SIZE, 2 * HEAD_SIZE), 2 * HEAD_SIZE)]
        dst = qbuf.at[n, pl.ds(my_rows, ROWS), :]
        copy = remote(src, dst, q_send.at[n, to], q_recv.at[n, me], member(to))
        if start:
            copy.start()
        else:
            copy.wait_send()

    def q_own(n):
        _, first = heads_of(me)
        src = q_in.at[:, pl.ds(pl.multiple_of((first + 2 * n) * HEAD_SIZE, 2 * HEAD_SIZE), 2 * HEAD_SIZE)]
        return pltpu.make_async_copy(src, qbuf.at[n, pl.ds(my_rows, ROWS), :], q_recv.at[n, me])

    def q_arrive(n, i):
        rows = pl.ds(pl.multiple_of(i * ROWS, ROWS), ROWS)
        pltpu.make_async_copy(qbuf.at[n, rows, :], qbuf.at[n, rows, :], q_recv.at[n, i]).wait()

    def loop(n, f, first=0):
        def body(i, _):
            f(i)
            return 0
        lax.fori_loop(first, n, body, 0)

    def piece(buf, slot, half):
        return buf.at[pl.ds(pl.multiple_of(slot * SUPER + half * HALF, HALF), HALF), :]

    def z_copy(d, part):
        buf = (kbuf, vbuf)[part]
        return remote(piece(buf, 2 * d, core), piece(buf, 2 * d + 2, core), z_send.at[part, d],
                      z_recv.at[part, d + 1], (after, head))

    def y_copy(i, part):
        buf = (kbuf, vbuf)[part]
        return remote(piece(buf, 2 * (i + yp), core), piece(buf, 2 * i + 1, core), y_send.at[part, i],
                      y_recv.at[part, i], (across, head))

    def s_copy(slot, part):
        buf = (kbuf, vbuf)[part]
        return remote(piece(buf, slot, core), piece(buf, slot, core), s_send.at[part, slot],
                      s_recv.at[part, slot], (ctx, other))

    def landed(slot, half, sem, part):
        buf = (kbuf, vbuf)[part]
        ref = piece(buf, slot, half)
        pltpu.make_async_copy(ref, ref, sem).wait()

    def back_copy(n):
        if n == 0:
            return remote(piece(kbuf, 0, core), around, b_send.at[0], b_recv.at[0], (back, head))
        return remote(around, piece(kbuf, 8, core), b_send.at[1], z_recv.at[0, 4], (back, head))

    def exists(slot):
        return 2 * z + yp >= slot

    def pass_on(d, parts=(0, 1)):
        @pl.when(exists(2 * d))
        def _():
            for part in parts:
                if d > 0:
                    landed(2 * d, core, z_recv.at[part, d], part)
                if d < 4:
                    @pl.when(z < LEVELS - 1)
                    def _():
                        z_copy(d, part).start()
                if d == 0:
                    @pl.when(yp == 0)
                    def _():
                        y_copy(0, part).start()
                elif d == 4:
                    @pl.when(yp == 1)
                    def _():
                        y_copy(3, part).start()
                else:
                    y_copy(d - yp, part).start()
                s_copy(2 * d, part).start()

    def pass_odd(i, parts=(0, 1)):
        @pl.when(exists(2 * i + 1))
        def _():
            for part in parts:
                landed(2 * i + 1, core, y_recv.at[part, i], part)
                s_copy(2 * i + 1, part).start()

    def whole(slot):
        @pl.when(exists(slot))
        def _():
            for part in (0, 1):
                landed(slot, 1 - core, s_recv.at[part, slot], part)

    def o_copy(n, i):
        to = lax.rem(me + i, 16)
        _, first = heads_of(me)
        src = obuf.at[n, pl.ds(pl.multiple_of(to * ROWS, ROWS), ROWS), :]
        dst = o_ref.at[:, pl.ds(pl.multiple_of((first + 2 * n) * HEAD_SIZE, 2 * HEAD_SIZE), 2 * HEAD_SIZE)]
        return remote(src, dst, o_send.at[n, to], o_recv.at[n, me], member(to))

    def o_own(n):
        _, first = heads_of(me)
        src = obuf.at[n, pl.ds(my_rows, ROWS), :]
        dst = o_ref.at[:, pl.ds(pl.multiple_of((first + 2 * n) * HEAD_SIZE, 2 * HEAD_SIZE), 2 * HEAD_SIZE)]
        return pltpu.make_async_copy(src, dst, o_recv.at[n, me])

    def o_arrive(n, i):
        _, first = heads_of(i)
        dst = o_ref.at[:, pl.ds(pl.multiple_of((first + 2 * n) * HEAD_SIZE, 2 * HEAD_SIZE), 2 * HEAD_SIZE)]
        pltpu.make_async_copy(dst, dst, o_recv.at[n, i]).wait()

    def o_send_pair(n):
        o_own(n).start()
        loop(16, lambda j: o_copy(n, j).start(), 1)

    for part in (0, 1):
        loop(8, lambda j: kv_copy(j, part, True))
    def q_send_pair(n):
        q_own(n).start()
        loop(16, lambda i: q_copy(n, i, True), 1)

    fetch[2].wait()
    q_send_pair(0)

    lane = lax.broadcasted_iota(jnp.int32, (1, HEAD_SIZE), 1)
    begins = jnp.where(lane == DOCS, -(1 << 20), 1 << 20)
    ends = jnp.where(lane == DOCS, 0, 1 << 20)
    total = jnp.int32(0)
    for j in range(DOCS):
        begins = jnp.where(lane == j, total, begins)
        total = total + doc_ref[j]
        ends = jnp.where(lane == j, total, ends)
    base = (z * 2 + yp) * SUPER

    def one_hot(first, count):
        position = first + lax.broadcasted_iota(jnp.int32, (count, HEAD_SIZE), 0)
        return (position >= begins) & (position < ends)

    qdoc[...] = jnp.where(one_hot(base, SUPER), 0.0, NEGATIVE).astype(jnp.bfloat16)

    def key_documents(slot):
        kdoc[pl.ds(pl.multiple_of(slot * SUPER, SUPER), SUPER), :] = jnp.where(
            one_hot(base - slot * SUPER, SUPER), 1.0, 0.0).astype(jnp.bfloat16)

    loop(SLOTS, key_documents)
    for slot in range(1, SLOTS):
        @pl.when(jnp.logical_not(exists(slot)))
        def _():
            for buf in (kbuf, vbuf):
                buf[pl.ds(slot * SUPER, SUPER), :] = jnp.zeros((SUPER, HEAD_SIZE), jnp.bfloat16)

    def attend(g, r, slots, kind):
        blocks = []
        for slot in slots:
            if slot == 0:
                blocks = [(0, r)] + ([(0, 0)] if r == 1 else []) + blocks
            elif slot == 8:
                blocks = [(8, r)] + ([(8, 1)] if r == 0 else []) + blocks
            else:
                blocks = blocks + [(slot, 0), (slot, 1)]
        keys = len(blocks) * HALF
        mine = pl.ds(r * HALF, HALF)

        def rows_of(ref):
            parts = [ref[pl.ds(slot * SUPER + half * HALF, HALF), :] for slot, half in blocks]
            return parts[0] if len(parts) == 1 else jnp.concatenate(parts, axis=0)

        q = jnp.concatenate(
            [qbuf[g // 2, mine, (g % 2) * HEAD_SIZE : (g % 2 + 1) * HEAD_SIZE], qdoc[mine, :]], axis=1)
        k = jnp.concatenate([rows_of(kbuf), rows_of(kdoc)], axis=1)
        v = jnp.concatenate([rows_of(vbuf), jnp.ones((keys, HEAD_SIZE), jnp.bfloat16)], axis=1)
        s = lax.dot_general(q, k, (((1,), (1,)), ((), ())), preferred_element_type=jnp.float32)
        if 0 in slots or 8 in slots:
            t = lax.broadcasted_iota(jnp.int32, (HALF, HALF), 0)
            u = lax.broadcasted_iota(jnp.int32, (HALF, HALF), 1)
            near = jnp.where(u <= t if 0 in slots else u > t, s[:, :HALF], NEGATIVE)
            s = near if keys == HALF else jnp.concatenate([near, s[:, HALF:]], axis=1)
        high = jnp.max(s, axis=1, keepdims=True)
        if kind != "first":
            old = top[g, mine, :1]
            high = jnp.maximum(high, old)
        p = jnp.exp2(s * SCALE2 - high * SCALE2).astype(jnp.bfloat16)
        part = jnp.dot(p, v, preferred_element_type=jnp.float32)
        if kind != "first":
            part = part + acc[g, mine, :] * jnp.exp2((old - high) * SCALE2)
        if kind == "last":
            obuf[g // 2, mine, (g % 2) * HEAD_SIZE : (g % 2 + 1) * HEAD_SIZE] = (
                part[:, :HEAD_SIZE] / part[:, HEAD_SIZE:]).astype(jnp.bfloat16)
        else:
            acc[g, mine, :] = part
            top[g, mine, :] = jnp.broadcast_to(high, (HALF, HEAD_SIZE))

    def pair(n, slots, kind="middle"):
        def run():
            for g in (2 * n, 2 * n + 1):
                for r in (0, 1):
                    attend(g, r, slots, kind)

        if kind == "middle":
            pl.when(exists(min(slots)))(run)
        else:
            run()

    loop(8, lambda j: kv_arrive(j, 0))
    pass_on(0, (0,))
    q_send_pair(1)
    loop(8, lambda j: kv_arrive(j, 1))
    pass_on(0, (1,))
    pass_on(1, (0,))
    whole(0)
    pass_on(1, (1,))
    loop(16, lambda i: q_arrive(0, i))
    pair(0, (0,), "first")
    pass_on(2, (0,))
    whole(2)
    pair(0, (2,))
    pass_on(2, (1,))
    pass_on(3, (0,))
    pass_odd(0)
    loop(16, lambda i: q_arrive(1, i))
    pair(1, (0, 2), "first")
    pass_on(3, (1,))
    pass_on(4, (0,))
    pass_odd(1, (0,))
    whole(1)
    whole(4)
    pair(0, (1, 4))
    pass_on(4, (1,))
    pass_odd(1, (1,))
    pass_odd(2, (0,))
    pair(1, (1, 4))
    pass_odd(2, (1,))
    pass_odd(3, (0,))
    whole(3)
    whole(6)
    pair(0, (3, 6))
    pass_odd(3, (1,))
    pair(1, (3, 6))
    whole(8)
    whole(5)
    whole(7)
    pair(0, (8, 5, 7), "last")
    o_send_pair(0)
    pair(1, (8, 5, 7), "last")
    o_send_pair(1)

    for part in (0, 1):
        loop(8, lambda j: kv_copy(j, part, False))
        for d in range(4):
            @pl.when(exists(2 * d) & (z < LEVELS - 1))
            def _():
                z_copy(d, part).wait_send()

            @pl.when(z >= d + yp)
            def _():
                y_copy(d, part).wait_send()
        for slot in range(SLOTS):
            @pl.when(exists(slot))
            def _():
                s_copy(slot, part).wait_send()
    for n in (0, 1):
        loop(16, lambda i: q_copy(n, i, False), 1)
    for n in (0, 1):
        loop(16, lambda j: o_copy(n, j).wait_send(), 1)
        loop(16, lambda i: o_arrive(n, i))


def on_device(token_queries, token_keys, token_values, doc_lengths):
    dma = pltpu.SemaphoreType.DMA
    any_space = pl.BlockSpec(memory_space=pl.ANY)
    return pl.pallas_call(
        kernel,
        name="packed_attention",
        out_shape=jax.ShapeDtypeStruct((ROWS, QUERY_HEADS * HEAD_SIZE), jnp.bfloat16),
        in_specs=[any_space] * 3 + [pl.BlockSpec(memory_space=pltpu.SMEM)],
        out_specs=any_space,
        scratch_shapes=[
            pltpu.VMEM((2, SUPER, 2 * HEAD_SIZE), jnp.bfloat16),
            pltpu.VMEM((SLOTS * SUPER, HEAD_SIZE), jnp.bfloat16),
            pltpu.VMEM((SLOTS * SUPER, HEAD_SIZE), jnp.bfloat16),
            pltpu.VMEM((SLOTS * SUPER, HEAD_SIZE), jnp.bfloat16),
            pltpu.VMEM((SUPER, HEAD_SIZE), jnp.bfloat16),
            pltpu.VMEM((HEADS, SUPER, 2 * HEAD_SIZE), jnp.float32),
            pltpu.VMEM((HEADS, SUPER, HEAD_SIZE), jnp.float32),
            pltpu.VMEM((2, SUPER, 2 * HEAD_SIZE), jnp.bfloat16),
            dma((2, 8)), dma((2, 8)), dma((2, 16)), dma((2, 16)),
            dma((2, 4)), dma((2, 5)), dma((2, 4)), dma((2, 4)),
            dma((2, SLOTS)), dma((2, SLOTS)), dma((2, 16)), dma((2, 16)),
            pltpu.VMEM((ROWS, QUERY_HEADS * HEAD_SIZE), jnp.bfloat16),
            pltpu.VMEM((ROWS, KEY_VALUE_HEADS * HEAD_SIZE), jnp.bfloat16),
            pltpu.VMEM((ROWS, KEY_VALUE_HEADS * HEAD_SIZE), jnp.bfloat16),
            dma((3,)),
        ],
        compiler_params=pltpu.CompilerParams(
            collective_id=0, has_side_effects=True, vmem_limit_bytes=63 * 2**20),
    )(token_queries, token_keys, token_values, doc_lengths)


def solution(mesh):
    in_specs = (P(("ctx", "head"), None), P(("ctx", "head"), None), P(("ctx", "head"), None), P())
    return jax.shard_map(
        on_device, mesh=mesh, in_specs=in_specs, out_specs=P(("ctx", "head"), None), check_vma=False
    )
```
